32 devices in a mesh: tm: 8 (over z, core), gz: 4 (over y, x).
Axes of the slice: x: 2, y: 2, z: 4, core: 2. Of those that a mesh axis runs over, the one named last changes fastest.
Arguments:
- c_states: float32 [8, 3, 16, 16, 256], P('tm', None, 'gz'), may hold values from -6 to 6
- velocity: float32 [3, 16, 16, 256], P(None, 'gz'), may hold values from -0.11 to 0.11
Outputs:
- updated: float32 [8, 3, 16, 16, 256], P('tm', None, 'gz')
The draws below stay inside these ranges and needn't reach their ends.
All inputs are finite; a program needn't handle non-finite values.
Results may differ from the reference program's by a relative error of at most 0.00002.
Values sent between devices are 32-bit elements; how exact they have to be, the bound alone decides.
A program may use at most 64 MiB of HBM per device.

```python
import jax
import jax.numpy as jnp
from jax import lax

X_CELLS = 16
Y_CELLS = 256
STEPS = 4
NZ = 16
INTERVALS = 8


def level_of(own_key, extent, pieces, low, top_value):
    loudness = 1.0
    for dim, parts in pieces:
        draws = jax.random.uniform(jax.random.fold_in(jax.random.fold_in(own_key, 6), dim), (parts,), jnp.float32, low / len(pieces), top_value / len(pieces))
        loudness = loudness * jnp.repeat(jnp.exp(draws), extent[dim] // parts).reshape((-1,) + (1,) * (len(extent) - 1 - dim))
    return loudness


def gaussian(own_key, dims, scale, reach, cuts=(), held_as=jnp.bfloat16):
    array = scale * jax.random.normal(own_key, dims, jnp.float32)
    if cuts:
        array = array * level_of(own_key, dims, cuts, -0.22, 0.18)
    return jnp.clip(array, -reach, reach).astype(held_as)


def setup_inputs(seed: int = 0) -> dict:
    arg_keys = jax.random.split(jax.random.key(seed), 3)
    c_states = gaussian(arg_keys[0], (INTERVALS, 3, NZ, X_CELLS, Y_CELLS), 1.0, 6.0, ((0, 8), (2, 4)), jnp.float32)
    velocity = jnp.clip(jax.random.uniform(arg_keys[1], (3, NZ, X_CELLS, Y_CELLS), jnp.float32, -0.11, 0.11) * level_of(arg_keys[1], (3, NZ, X_CELLS, Y_CELLS), ((1, 4),), -0.4, 0.0), -0.11, 0.11)
    return dict(c_states=c_states, velocity=velocity)


KAPPA = 0.04


def pad_space(values):
    return jnp.pad(values, ((0, 0), (1, 1), (1, 1), (1, 1)))


def neighbours(padded, direction):
    lower_cut = [slice(None), slice(1, -1), slice(1, -1), slice(1, -1)]
    upper_cut = list(lower_cut)
    lower_cut[direction] = slice(0, -2)
    upper_cut[direction] = slice(2, None)
    return padded[tuple(lower_cut)], padded[tuple(upper_cut)]


def tensor_of(courant):
    padded = pad_space(courant)
    columns = []
    for direction in (1, 2, 3):
        lower_side, upper_side = neighbours(padded, direction)
        columns.append((upper_side - lower_side) * 0.5)
    return jnp.stack(columns, axis=1)


def march_padded(padded, courant, tensor):
    middle = padded[:, 1:-1, 1:-1, 1:-1]
    advection = jnp.zeros_like(middle)
    laplace = jnp.zeros_like(middle)
    for direction in (1, 2, 3):
        lower_side, upper_side = neighbours(padded, direction)
        speed = courant[direction - 1][None]
        advection = advection + jnp.maximum(speed, 0.0) * (middle - lower_side) + jnp.minimum(speed, 0.0) * (upper_side - middle)
        laplace = laplace + upper_side + lower_side - 2.0 * middle
    stretch = tensor[:, 0] * middle[0:1] + tensor[:, 1] * middle[1:2] + tensor[:, 2] * middle[2:3]
    return middle - advection + stretch + KAPPA * laplace


def march(current, courant, tensor):
    return march_padded(pad_space(current), courant, tensor)


def coarsen(values):
    comps, zlen, xlen, ylen = values.shape
    return values.reshape(comps, zlen // 2, 2, xlen // 2, 2, ylen // 2, 2).mean(axis=(2, 4, 6))


def refine(values):
    return jnp.repeat(jnp.repeat(jnp.repeat(values, 2, 1), 2, 2), 2, 3)


def reference(c_states, velocity):
    tensor = tensor_of(velocity)
    coarse_speed = 2.0 * coarsen(velocity)
    coarse_tensor = tensor_of(coarse_speed)

    def propagate(start_state):
        current = start_state
        for _ in range(STEPS):
            current = march(current, velocity, tensor)
        return current

    stepped = lax.map(propagate, c_states)
    relaxed = jnp.concatenate([c_states[:1], stepped[:-1]], axis=0)
    again = lax.map(propagate, relaxed)
    coarse_relaxed = lax.map(coarsen, relaxed)
    coarse_again = lax.map(coarsen, again)

    def psi_of(field):
        return march(field, coarse_speed, coarse_tensor)

    forcing = coarse_again[:-1] - lax.map(psi_of, coarse_relaxed[:-1])

    def sweep(state, source):
        following = march(state, coarse_speed, coarse_tensor) + source
        return following, following

    first = coarse_relaxed[0]
    final_state, states = lax.scan(sweep, first, forcing)
    states = jnp.concatenate([first[None], states], axis=0)
    return relaxed + lax.map(refine, states - coarse_relaxed)
```

```python
import functools

import jax
import jax.numpy as jnp
from jax import lax
from jax.experimental import pallas as pl
from jax.experimental.pallas import tpu as pltpu
from jax.sharding import PartitionSpec as P

STEPS = 4
KAPPA = 0.04
LANES = 128
MESH = pl.DeviceIdType.MESH


def kernel(
    intervals, slabs, offset,
    c_ref, v_ref, out_ref,
    v_win, c_win, speed, field_a, field_b, relaxed, cf, speed_c, cf_c,
    pairs, r_relaxed, r_again, delta, sent, got, rel_slab, delta_slab, fine_tmp,
    v_send, v_recv, c_send, c_recv, c0_send, r_send, r_recv, d_send, d_recv, f_send, f_recv,
):
    t = lax.axis_index("tm")
    me = lax.axis_index("gz")
    first_t = t == 0
    last_t = t == intervals - 1
    zs, rows, y_all = v_ref.shape[1:]
    core = y_all // slabs
    depth = zs * slabs
    half = depth // 2
    zsc = zs // 2
    lanes = v_win.shape[-1]

    barrier = pltpu.get_barrier_semaphore()
    for g in range(slabs):
        @pl.when(me != g)
        def _():
            pl.semaphore_signal(barrier, inc=1, device_id=(t, g), device_id_type=MESH)

        @pl.when(jnp.logical_not(first_t))
        def _():
            pl.semaphore_signal(barrier, inc=1, device_id=(t - 1, g), device_id_type=MESH)

        @pl.when(jnp.logical_not(last_t))
        def _():
            pl.semaphore_signal(barrier, inc=1, device_id=(t + 1, g), device_id_type=MESH)

    def cut(read, target):
        def layer(z, carry):
            for c in range(3):
                whole = read(c, z)
                for g in range(slabs):
                    shift = (offset - g * core) % y_all
                    turned = pltpu.roll(whole, shift, 1) if shift else whole
                    target[g, c, z] = turned[:, :lanes]
            return carry

        lax.fori_loop(0, zs, layer, 0)

    cut(lambda c, z: v_ref[c, z], v_win)
    nothing = jnp.zeros((rows, lanes), jnp.float32)
    nothing_c = jnp.zeros((rows // 2, lanes), jnp.float32)
    for c in range(3):
        for ref in (speed, field_a, field_b, relaxed):
            ref[c, 0] = nothing
            ref[c, depth + 1] = nothing
        for ref in (speed_c, delta):
            ref[c, 0] = nothing_c
            ref[c, half + 1] = nothing_c

    sides = 2 - first_t.astype(jnp.int32) - last_t.astype(jnp.int32)
    pl.semaphore_wait(barrier, slabs - 1 + slabs * sides)

    def slab_of(ref, g, width):
        return ref.at[:, pl.ds(1 + g * width, width)]

    def v_copy(g, slot):
        return pltpu.make_async_remote_copy(
            v_win.at[g], slab_of(speed, slot, zs), v_send.at[g], v_recv.at[slot],
            device_id=(t, g), device_id_type=MESH)

    def c_copy(g, slot, target, sem):
        return pltpu.make_async_remote_copy(
            c_win.at[g], slab_of(field_a, slot, zs), sem.at[g], c_recv.at[slot],
            device_id=(target, g), device_id_type=MESH)

    def r_copy(g, slot):
        return pltpu.make_async_remote_copy(
            slab_of(relaxed, g, zs), rel_slab.at[slot], r_send.at[g], r_recv.at[slot],
            device_id=(t, g), device_id_type=MESH)

    def d_copy(g, slot):
        return pltpu.make_async_remote_copy(
            slab_of(delta, g, zsc), delta_slab.at[slot], d_send.at[g], d_recv.at[slot],
            device_id=(t, g), device_id_type=MESH)

    f_copy = pltpu.make_async_remote_copy(
        sent.at[:, pl.ds(1, half)], got, f_send, f_recv,
        device_id=(t + 1, me), device_id_type=MESH)

    for g in range(slabs):
        @pl.when(me != g)
        def _():
            v_copy(g, me).start()

    cut(lambda c, z: c_ref[0, c, z], c_win)
    for g in range(slabs):
        @pl.when(jnp.logical_not(last_t))
        def _():
            c_copy(g, me, t + 1, c_send).start()

        @pl.when(jnp.logical_and(first_t, me != g))
        def _():
            c_copy(g, me, t, c0_send).start()

        @pl.when(me == g)
        def _():
            speed[:, 1 + g * zs : 1 + (g + 1) * zs] = v_win[g]

            @pl.when(first_t)
            def _():
                field_a[:, 1 + g * zs : 1 + (g + 1) * zs] = c_win[g]

    lane = lax.broadcasted_iota(jnp.int32, (rows, lanes), 1)
    even = lane % 2 == 0
    cell = lax.rem(lane + me * core - offset + y_all, y_all)

    def coefficients(vel, cf, n, ys):
        height = vel.shape[-2]
        row = lax.broadcasted_iota(jnp.int32, (height, lanes), 0)
        y = cell[:height]
        x_low = (row > 0).astype(jnp.float32)
        x_high = (row < height - 1).astype(jnp.float32)
        y_low = (y >= ys).astype(jnp.float32)
        y_high = (y < y_all - ys).astype(jnp.float32)

        def layer(z, carry):
            u = [vel[d, z + 1] for d in range(3)]
            low = [jnp.maximum(a, 0.0) + KAPPA for a in u]
            high = [KAPPA - jnp.minimum(a, 0.0) for a in u]
            cf[0, z] = low[0]
            cf[1, z] = high[0]
            cf[2, z] = low[1] * x_low
            cf[3, z] = high[1] * x_high
            cf[4, z] = low[2] * y_low
            cf[5, z] = high[2] * y_high
            centre = (1.0 - 6.0 * KAPPA) - (jnp.abs(u[0]) + jnp.abs(u[1]) + jnp.abs(u[2]))
            for c in range(3):
                grad = [
                    (vel[c, z + 2] - vel[c, z]) * 0.5,
                    (pltpu.roll(u[c], height - 1, 0) * x_high - pltpu.roll(u[c], 1, 0) * x_low) * 0.5,
                    (pltpu.roll(u[c], lanes - ys, 1) * y_high - pltpu.roll(u[c], ys, 1) * y_low) * 0.5,
                ]
                for d in range(3):
                    cf[6 + 3 * c + d, z] = grad[d] + centre if d == c else grad[d]
            return carry

        lax.fori_loop(0, n, layer, 0)

    def march(src, dst, cf, n, ys, unroll, extra=None):
        height = src.shape[-2]

        def layers(block, carry):
            for k in range(unroll):
                z = block * unroll + k
                w = [src[c, z + 1] for c in range(3)]
                a = [cf[i, z] for i in range(6)]
                for c in range(3):
                    new = cf[6 + 3 * c, z] * w[0] + cf[7 + 3 * c, z] * w[1] + cf[8 + 3 * c, z] * w[2]
                    new = new + (a[0] * src[c, z] + a[1] * src[c, z + 2])
                    new = new + (a[2] * pltpu.roll(w[c], 1, 0) + a[3] * pltpu.roll(w[c], height - 1, 0))
                    new = new + (a[4] * pltpu.roll(w[c], ys, 1) + a[5] * pltpu.roll(w[c], lanes - ys, 1))
                    if extra is not None:
                        new = new + extra[c, z + 1]
                    dst[c, z + 1] = new
            return carry

        lax.fori_loop(0, n // unroll, layers, 0)

    def restrict(src, dst, scale):
        def layer(z, carry):
            for c in range(3):
                both = src[c, 2 * z + 1] + src[c, 2 * z + 2]
                both = both + jnp.where(even, pltpu.roll(both, lanes - 1, 1), pltpu.roll(both, 1, 1))
                for part in range(lanes // LANES):
                    at = slice(part * LANES, (part + 1) * LANES)
                    pairs[part, c, z] = both[:, at]
            for c in range(3):
                for part in range(lanes // LANES):
                    at = slice(part * LANES, (part + 1) * LANES)
                    dst[c, z + 1, :, at] = scale * (
                        pairs[part, c, z, pl.ds(0, rows // 2, stride=2), :]
                        + pairs[part, c, z, pl.ds(1, rows // 2, stride=2), :])
            return carry

        lax.fori_loop(0, half, layer, 0)

    for g in range(slabs):
        @pl.when(me != g)
        def _():
            v_copy(g, g).wait_recv()

    coefficients(speed, cf, depth, 1)
    restrict(speed, speed_c, 0.25)
    coefficients(speed_c, cf_c, half, 2)

    for g in range(slabs):
        @pl.when(jnp.logical_or(jnp.logical_not(first_t), me != g))
        def _():
            c_copy(g, g, t, c_send).wait_recv()

    @pl.when(first_t)
    def _():
        relaxed[...] = field_a[...]

    @pl.when(jnp.logical_not(first_t))
    def _():
        march(field_a, field_b, cf, depth, 1, 2)
        march(field_b, field_a, cf, depth, 1, 2)
        march(field_a, field_b, cf, depth, 1, 2)
        march(field_b, relaxed, cf, depth, 1, 2)

    for g in range(slabs):
        @pl.when(me != g)
        def _():
            r_copy(g, me).start()

        @pl.when(me == g)
        def _():
            rel_slab[g] = relaxed[:, 1 + g * zs : 1 + (g + 1) * zs]

    march(relaxed, field_b, cf, depth, 1, 2)
    march(field_b, field_a, cf, depth, 1, 2)
    march(field_a, field_b, cf, depth, 1, 2)
    march(field_b, field_a, cf, depth, 1, 2)
    restrict(field_a, r_again, 0.125)
    restrict(relaxed, r_relaxed, 0.125)

    @pl.when(first_t)
    def _():
        delta[:, 1 : half + 1] = jnp.zeros((3, half, rows // 2, lanes), jnp.float32)

    @pl.when(jnp.logical_not(first_t))
    def _():
        f_copy.wait_recv()
        delta[:, 1 : half + 1] = got[...] - r_relaxed[:, 1 : half + 1]

    @pl.when(jnp.logical_not(last_t))
    def _():
        march(delta, sent, cf_c, half, 2, 2, r_again)
        f_copy.start()

    for g in range(slabs):
        @pl.when(me != g)
        def _():
            d_copy(g, me).start()

        @pl.when(me == g)
        def _():
            delta_slab[g] = delta[:, 1 + g * zsc : 1 + (g + 1) * zsc]

    tile_lane = lax.broadcasted_iota(jnp.int32, (rows, LANES), 1)

    def joined(read, tile):
        total = None
        for g in range(slabs):
            start = g * core - tile * LANES
            if start < 0 or start >= LANES:
                continue
            shift = (start - offset) % lanes
            piece = read(g)
            piece = pltpu.roll(piece, shift, 1) if shift else piece
            piece = piece[:, :LANES]
            total = piece if total is None else jnp.where(tile_lane[: piece.shape[0]] >= start, piece, total)
        return total

    for g in range(slabs):
        @pl.when(me != g)
        def _():
            r_copy(g, g).wait_recv()

    def rel_layer(z, carry):
        for c in range(3):
            for tile in range(y_all // LANES):
                out_ref[0, c, z, :, tile * LANES : (tile + 1) * LANES] = joined(lambda g: rel_slab[g, c, z], tile)
        return carry

    lax.fori_loop(0, zs, rel_layer, 0)

    for g in range(slabs):
        @pl.when(me != g)
        def _():
            d_copy(g, g).wait_recv()

    def out_layer(z, carry):
        for c in range(3):
            for tile in range(y_all // LANES):
                at = slice(tile * LANES, (tile + 1) * LANES)
                coarse = joined(lambda g: delta_slab[g, c, z], tile)
                fine_tmp[tile, c, z, pl.ds(0, rows // 2, stride=2), :] = coarse
                fine_tmp[tile, c, z, pl.ds(1, rows // 2, stride=2), :] = coarse
            for tile in range(y_all // LANES):
                at = slice(tile * LANES, (tile + 1) * LANES)
                fine = fine_tmp[tile, c, z]
                for k in range(2):
                    out_ref[0, c, 2 * z + k, :, at] = out_ref[0, c, 2 * z + k, :, at] + fine
        return carry

    lax.fori_loop(0, zsc, out_layer, 0)

    for g in range(slabs):
        @pl.when(me != g)
        def _():
            v_copy(g, me).wait_send()
            r_copy(g, me).wait_send()
            d_copy(g, me).wait_send()

        @pl.when(jnp.logical_not(last_t))
        def _():
            c_copy(g, me, t + 1, c_send).wait_send()

        @pl.when(jnp.logical_and(first_t, me != g))
        def _():
            c_copy(g, me, t, c0_send).wait_send()

    @pl.when(jnp.logical_not(last_t))
    def _():
        f_copy.wait_send()


def local(c_states, velocity):
    intervals = lax.axis_size("tm")
    slabs = lax.axis_size("gz")
    zs, rows, y_all = velocity.shape[1:]
    core = y_all // slabs
    depth = zs * slabs
    half = depth // 2
    halo = 2 * STEPS + 2 * (intervals - 1)
    lanes = min(y_all, -(-(core + 2 * halo) // LANES) * LANES)
    offset = (lanes - core) // 4 * 2
    f32 = jnp.float32
    windows = pltpu.VMEM((slabs, 3, zs, rows, lanes), f32)
    field = pltpu.VMEM((3, depth + 2, rows, lanes), f32)
    coarse = pltpu.VMEM((3, half + 2, rows // 2, lanes), f32)
    several = pltpu.SemaphoreType.DMA((slabs,))
    one = pltpu.SemaphoreType.DMA
    return pl.pallas_call(
        functools.partial(kernel, intervals, slabs, offset),
        out_shape=jax.ShapeDtypeStruct(c_states.shape, f32),
        in_specs=[pl.BlockSpec(memory_space=pltpu.VMEM)] * 2,
        out_specs=pl.BlockSpec(memory_space=pltpu.VMEM),
        scratch_shapes=[
            windows, windows, field, field, field, field,
            pltpu.VMEM((15, depth, rows, lanes), f32),
            coarse,
            pltpu.VMEM((15, half, rows // 2, lanes), f32),
            pltpu.VMEM((lanes // LANES, 3, half, rows, LANES), f32),
            coarse, coarse, coarse, coarse,
            pltpu.VMEM((3, half, rows // 2, lanes), f32),
            windows,
            pltpu.VMEM((slabs, 3, zs // 2, rows // 2, lanes), f32),
            pltpu.VMEM((y_all // LANES, 3, zs // 2, rows, LANES), f32),
            several, several, several, several, several, several, several, several, several,
            one, one,
        ],
        compiler_params=pltpu.CompilerParams(
            collective_id=0, has_side_effects=True, vmem_limit_bytes=56 * 2**20
        ),
    )(c_states, velocity)


def solution(mesh):
    return jax.shard_map(
        local,
        mesh=mesh,
        in_specs=(P("tm", None, "gz", None, None), P(None, "gz", None, None)),
        out_specs=P("tm", None, "gz", None, None),
        check_vma=False,
    )
```

```python
import functools

import jax
import jax.numpy as jnp
from jax import lax
from jax.experimental import pallas as pl
from jax.experimental.pallas import tpu as pltpu
from jax.sharding import PartitionSpec as P

STEPS = 4
KAPPA = 0.04
LANES = 128
MESH = pl.DeviceIdType.MESH


def kernel(
    intervals, slabs, offset,
    c_ref, v_ref, out_ref,
    v_win, c_win, speed, field_a, field_b, relaxed, cf, speed_c, cf_c,
    pairs, r_relaxed, r_again, delta, sent, got, rel_slab, delta_slab, fine_tmp,
    v_send, v_recv, c_send, c_recv, c0_send, r_send, r_recv, d_send, d_recv, f_send, f_recv,
):
    t = lax.axis_index("tm")
    me = lax.axis_index("gz")
    first_t = t == 0
    last_t = t == intervals - 1
    zs, rows, y_all = v_ref.shape[1:]
    core = y_all // slabs
    depth = zs * slabs
    half = depth // 2
    zsc = zs // 2
    lanes = v_win.shape[-1]

    barrier = pltpu.get_barrier_semaphore()
    for g in range(slabs):
        @pl.when(me != g)
        def _():
            pl.semaphore_signal(barrier, inc=1, device_id=(t, g), device_id_type=MESH)

        @pl.when(jnp.logical_not(first_t))
        def _():
            pl.semaphore_signal(barrier, inc=1, device_id=(t - 1, g), device_id_type=MESH)

        @pl.when(jnp.logical_not(last_t))
        def _():
            pl.semaphore_signal(barrier, inc=1, device_id=(t + 1, g), device_id_type=MESH)

    def cut(read, target):
        def layer(z, carry):
            for c in range(3):
                whole = read(c, z)
                for g in range(slabs):
                    shift = (offset - g * core) % y_all
                    turned = pltpu.roll(whole, shift, 1) if shift else whole
                    target[g, c, z] = turned[:, :lanes]
            return carry

        lax.fori_loop(0, zs, layer, 0)

    cut(lambda c, z: v_ref[c, z], v_win)
    nothing = jnp.zeros((rows, lanes), jnp.float32)
    nothing_c = jnp.zeros((rows // 2, lanes), jnp.float32)
    for c in range(3):
        for ref in (speed, field_a, field_b, relaxed):
            ref[c, 0] = nothing
            ref[c, depth + 1] = nothing
        for ref in (speed_c, delta):
            ref[c, 0] = nothing_c
            ref[c, half + 1] = nothing_c

    sides = 2 - first_t.astype(jnp.int32) - last_t.astype(jnp.int32)
    pl.semaphore_wait(barrier, slabs - 1 + slabs * sides)

    def slab_of(ref, g, width):
        return ref.at[:, pl.ds(1 + g * width, width)]

    def v_copy(g, slot):
        return pltpu.make_async_remote_copy(
            v_win.at[g], slab_of(speed, slot, zs), v_send.at[g], v_recv.at[slot],
            device_id=(t, g), device_id_type=MESH)

    def c_copy(g, slot, target, sem):
        return pltpu.make_async_remote_copy(
            c_win.at[g], slab_of(field_a, slot, zs), sem.at[g], c_recv.at[slot],
            device_id=(target, g), device_id_type=MESH)

    def r_copy(g, slot):
        return pltpu.make_async_remote_copy(
            slab_of(relaxed, g, zs), rel_slab.at[slot], r_send.at[g], r_recv.at[slot],
            device_id=(t, g), device_id_type=MESH)

    def d_copy(g, slot):
        return pltpu.make_async_remote_copy(
            slab_of(delta, g, zsc), delta_slab.at[slot], d_send.at[g], d_recv.at[slot],
            device_id=(t, g), device_id_type=MESH)

    def f_copy(z):
        return pltpu.make_async_remote_copy(
            sent.at[:, z], got.at[:, z], f_send.at[z], f_recv.at[z],
            device_id=(t + 1, me), device_id_type=MESH)

    for g in range(slabs):
        @pl.when(me != g)
        def _():
            v_copy(g, me).start()

    cut(lambda c, z: c_ref[0, c, z], c_win)
    for g in range(slabs):
        @pl.when(jnp.logical_not(last_t))
        def _():
            c_copy(g, me, t + 1, c_send).start()

        @pl.when(jnp.logical_and(first_t, me != g))
        def _():
            c_copy(g, me, t, c0_send).start()

        @pl.when(me == g)
        def _():
            speed[:, 1 + g * zs : 1 + (g + 1) * zs] = v_win[g]

            @pl.when(first_t)
            def _():
                field_a[:, 1 + g * zs : 1 + (g + 1) * zs] = c_win[g]

    lane = lax.broadcasted_iota(jnp.int32, (rows, lanes), 1)
    even = lane % 2 == 0
    cell = lax.rem(lane + me * core - offset + y_all, y_all)

    def coefficients(vel, cf, n, ys):
        height = vel.shape[-2]
        row = lax.broadcasted_iota(jnp.int32, (height, lanes), 0)
        y = cell[:height]
        x_low = (row > 0).astype(jnp.float32)
        x_high = (row < height - 1).astype(jnp.float32)
        y_low = (y >= ys).astype(jnp.float32)
        y_high = (y < y_all - ys).astype(jnp.float32)

        def layer(z, carry):
            u = [vel[d, z + 1] for d in range(3)]
            low = [jnp.maximum(a, 0.0) + KAPPA for a in u]
            high = [KAPPA - jnp.minimum(a, 0.0) for a in u]
            cf[0, z] = low[0]
            cf[1, z] = high[0]
            cf[2, z] = low[1] * x_low
            cf[3, z] = high[1] * x_high
            cf[4, z] = low[2] * y_low
            cf[5, z] = high[2] * y_high
            centre = (1.0 - 6.0 * KAPPA) - (jnp.abs(u[0]) + jnp.abs(u[1]) + jnp.abs(u[2]))
            for c in range(3):
                grad = [
                    (vel[c, z + 2] - vel[c, z]) * 0.5,
                    (pltpu.roll(u[c], height - 1, 0) * x_high - pltpu.roll(u[c], 1, 0) * x_low) * 0.5,
                    (pltpu.roll(u[c], lanes - ys, 1) * y_high - pltpu.roll(u[c], ys, 1) * y_low) * 0.5,
                ]
                for d in range(3):
                    cf[6 + 3 * c + d, z] = grad[d] + centre if d == c else grad[d]
            return carry

        lax.fori_loop(0, n, layer, 0)

    def march_layer(src, put, cf, z, ys, extra=None):
        height = src.shape[-2]
        w = [src[c, z + 1] for c in range(3)]
        a = [cf[i, z] for i in range(6)]
        for c in range(3):
            new = cf[6 + 3 * c, z] * w[0] + cf[7 + 3 * c, z] * w[1] + cf[8 + 3 * c, z] * w[2]
            new = new + (a[0] * src[c, z] + a[1] * src[c, z + 2])
            new = new + (a[2] * pltpu.roll(w[c], 1, 0) + a[3] * pltpu.roll(w[c], height - 1, 0))
            new = new + (a[4] * pltpu.roll(w[c], ys, 1) + a[5] * pltpu.roll(w[c], lanes - ys, 1))
            put(c, new)

    def march(src, dst, n, unroll):
        def layers(block, carry):
            for k in range(unroll):
                z = block * unroll + k

                def put(c, new):
                    dst[c, z + 1] = new

                march_layer(src, put, cf, z, 1)
            return carry

        lax.fori_loop(0, n // unroll, layers, 0)

    def restrict(src, dst, scale):
        def layer(z, carry):
            for c in range(3):
                both = src[c, 2 * z + 1] + src[c, 2 * z + 2]
                both = both + jnp.where(even, pltpu.roll(both, lanes - 1, 1), pltpu.roll(both, 1, 1))
                for part in range(lanes // LANES):
                    at = slice(part * LANES, (part + 1) * LANES)
                    pairs[part, c, z] = both[:, at]
            for c in range(3):
                for part in range(lanes // LANES):
                    at = slice(part * LANES, (part + 1) * LANES)
                    dst[c, z + 1, :, at] = scale * (
                        pairs[part, c, z, pl.ds(0, rows // 2, stride=2), :]
                        + pairs[part, c, z, pl.ds(1, rows // 2, stride=2), :])
            return carry

        lax.fori_loop(0, half, layer, 0)

    for g in range(slabs):
        @pl.when(me != g)
        def _():
            v_copy(g, g).wait_recv()

    coefficients(speed, cf, depth, 1)
    restrict(speed, speed_c, 0.25)
    coefficients(speed_c, cf_c, half, 2)

    for g in range(slabs):
        @pl.when(jnp.logical_or(jnp.logical_not(first_t), me != g))
        def _():
            c_copy(g, g, t, c_send).wait_recv()

    @pl.when(first_t)
    def _():
        relaxed[...] = field_a[...]

    @pl.when(jnp.logical_not(first_t))
    def _():
        march(field_a, field_b, depth, 2)
        march(field_b, field_a, depth, 2)
        march(field_a, field_b, depth, 2)
        march(field_b, relaxed, depth, 2)

    for g in range(slabs):
        @pl.when(me != g)
        def _():
            r_copy(g, me).start()

        @pl.when(me == g)
        def _():
            rel_slab[g] = relaxed[:, 1 + g * zs : 1 + (g + 1) * zs]

    march(relaxed, field_b, depth, 2)
    march(field_b, field_a, depth, 2)
    march(field_a, field_b, depth, 2)
    march(field_b, field_a, depth, 2)
    restrict(field_a, r_again, 0.125)
    restrict(relaxed, r_relaxed, 0.125)

    @pl.when(first_t)
    def _():
        delta[:, 1 : half + 1] = jnp.zeros((3, half, rows // 2, lanes), jnp.float32)

    def send_on(z):
        @pl.when(jnp.logical_not(last_t))
        def _():
            def put(c, new):
                sent[c, z] = new + r_again[c, z + 1]

            march_layer(delta, put, cf_c, z, 2)
            f_copy(z).start()

    for z in range(half):
        @pl.when(jnp.logical_not(first_t))
        def _():
            f_copy(z).wait_recv()
            delta[:, z + 1] = got[:, z] - r_relaxed[:, z + 1]

        if z > 0:
            send_on(z - 1)
        if z % zsc == zsc - 1:
            g = z // zsc

            @pl.when(me != g)
            def _():
                d_copy(g, me).start()

            @pl.when(me == g)
            def _():
                delta_slab[g] = delta[:, 1 + g * zsc : 1 + (g + 1) * zsc]
    send_on(half - 1)

    tile_lane = lax.broadcasted_iota(jnp.int32, (rows, LANES), 1)

    def joined(read, tile):
        total = None
        for g in range(slabs):
            start = g * core - tile * LANES
            if start < 0 or start >= LANES:
                continue
            shift = (start - offset) % lanes
            piece = read(g)
            piece = pltpu.roll(piece, shift, 1) if shift else piece
            piece = piece[:, :LANES]
            total = piece if total is None else jnp.where(tile_lane[: piece.shape[0]] >= start, piece, total)
        return total

    for g in range(slabs):
        @pl.when(me != g)
        def _():
            r_copy(g, g).wait_recv()

    def rel_layer(z, carry):
        for c in range(3):
            for tile in range(y_all // LANES):
                out_ref[0, c, z, :, tile * LANES : (tile + 1) * LANES] = joined(lambda g: rel_slab[g, c, z], tile)
        return carry

    lax.fori_loop(0, zs, rel_layer, 0)

    for g in range(slabs):
        @pl.when(me != g)
        def _():
            d_copy(g, g).wait_recv()

    def out_layer(z, carry):
        for c in range(3):
            for tile in range(y_all // LANES):
                at = slice(tile * LANES, (tile + 1) * LANES)
                coarse = joined(lambda g: delta_slab[g, c, z], tile)
                fine_tmp[tile, c, z, pl.ds(0, rows // 2, stride=2), :] = coarse
                fine_tmp[tile, c, z, pl.ds(1, rows // 2, stride=2), :] = coarse
            for tile in range(y_all // LANES):
                at = slice(tile * LANES, (tile + 1) * LANES)
                fine = fine_tmp[tile, c, z]
                for k in range(2):
                    out_ref[0, c, 2 * z + k, :, at] = out_ref[0, c, 2 * z + k, :, at] + fine
        return carry

    lax.fori_loop(0, zsc, out_layer, 0)

    for g in range(slabs):
        @pl.when(me != g)
        def _():
            v_copy(g, me).wait_send()
            r_copy(g, me).wait_send()
            d_copy(g, me).wait_send()

        @pl.when(jnp.logical_not(last_t))
        def _():
            c_copy(g, me, t + 1, c_send).wait_send()

        @pl.when(jnp.logical_and(first_t, me != g))
        def _():
            c_copy(g, me, t, c0_send).wait_send()

    @pl.when(jnp.logical_not(last_t))
    def _():
        for z in range(half):
            f_copy(z).wait_send()


def local(c_states, velocity):
    intervals = lax.axis_size("tm")
    slabs = lax.axis_size("gz")
    zs, rows, y_all = velocity.shape[1:]
    core = y_all // slabs
    depth = zs * slabs
    half = depth // 2
    halo = 2 * STEPS + 2 * (intervals - 1)
    lanes = min(y_all, -(-(core + 2 * halo) // LANES) * LANES)
    offset = (lanes - core) // 4 * 2
    f32 = jnp.float32
    windows = pltpu.VMEM((slabs, 3, zs, rows, lanes), f32)
    field = pltpu.VMEM((3, depth + 2, rows, lanes), f32)
    coarse = pltpu.VMEM((3, half + 2, rows // 2, lanes), f32)
    flat = pltpu.VMEM((3, half, rows // 2, lanes), f32)
    layered = pltpu.SemaphoreType.DMA((half,))
    several = pltpu.SemaphoreType.DMA((slabs,))
    return pl.pallas_call(
        functools.partial(kernel, intervals, slabs, offset),
        out_shape=jax.ShapeDtypeStruct(c_states.shape, f32),
        in_specs=[pl.BlockSpec(memory_space=pltpu.VMEM)] * 2,
        out_specs=pl.BlockSpec(memory_space=pltpu.VMEM),
        scratch_shapes=[
            windows, windows, field, field, field, field,
            pltpu.VMEM((15, depth, rows, lanes), f32),
            coarse,
            pltpu.VMEM((15, half, rows // 2, lanes), f32),
            pltpu.VMEM((lanes // LANES, 3, half, rows, LANES), f32),
            coarse, coarse, coarse, flat, flat,
            windows,
            pltpu.VMEM((slabs, 3, zs // 2, rows // 2, lanes), f32),
            pltpu.VMEM((y_all // LANES, 3, zs // 2, rows, LANES), f32),
            several, several, several, several, several, several, several, several, several,
            layered, layered,
        ],
        compiler_params=pltpu.CompilerParams(
            collective_id=0, has_side_effects=True, vmem_limit_bytes=56 * 2**20
        ),
    )(c_states, velocity)


def solution(mesh):
    return jax.shard_map(
        local,
        mesh=mesh,
        in_specs=(P("tm", None, "gz", None, None), P(None, "gz", None, None)),
        out_specs=P("tm", None, "gz", None, None),
        check_vma=False,
    )
```

```python
import functools

import jax
import jax.numpy as jnp
from jax import lax
from jax.experimental import pallas as pl
from jax.experimental.pallas import tpu as pltpu
from jax.sharding import PartitionSpec as P

STEPS = 4
KAPPA = 0.04
LANES = 128
MESH = pl.DeviceIdType.MESH


def kernel(
    intervals, slabs, offset,
    c_hbm, v_hbm, out_ref,
    c_ref, v_ref, v_win, c_win, speed, field_a, field_b, relaxed, cf, speed_c, cf_c,
    pairs, r_relaxed, r_again, delta, sent, got, rel_slab, delta_slab, fine_tmp,
    in_sem, v_send, v_recv, s_send, s_recv, c_send, c_recv, w_send, w_recv, r_send, r_recv, d_send, d_recv, f_send, f_recv,
):
    t = lax.axis_index("tm")
    me = lax.axis_index("gz")
    first_t = t == 0
    last_t = t == intervals - 1
    zs, rows, y_all = v_ref.shape[1:]
    core = y_all // slabs
    depth = zs * slabs
    half = depth // 2
    zsc = zs // 2
    lanes = v_win.shape[-1]

    v_in = pltpu.make_async_copy(v_hbm, v_ref, in_sem.at[0])
    c_in = pltpu.make_async_copy(c_hbm, c_ref, in_sem.at[1])
    v_in.start()
    c_in.start()
    core_index = t % 2
    sibling = t + 1 - 2 * core_index

    barrier = pltpu.get_barrier_semaphore()
    for g in range(slabs):
        @pl.when(me != g)
        def _():
            pl.semaphore_signal(barrier, inc=1, device_id=(t, g), device_id_type=MESH)

        @pl.when(jnp.logical_not(first_t))
        def _():
            pl.semaphore_signal(barrier, inc=1, device_id=(t - 1, g), device_id_type=MESH)

        @pl.when(jnp.logical_not(last_t))
        def _():
            pl.semaphore_signal(barrier, inc=1, device_id=(t + 1, g), device_id_type=MESH)

    def cut(read, target):
        def layer(z, carry):
            for c in range(3):
                whole = read(c, z)
                for g in range(slabs):
                    shift = (offset - g * core) % y_all
                    turned = pltpu.roll(whole, shift, 1) if shift else whole
                    target[g, c, z] = turned[:, :lanes]
            return carry

        lax.fori_loop(0, zs, layer, 0)

    v_in.wait()
    cut(lambda c, z: v_ref[c, z], v_win)
    nothing = jnp.zeros((rows, lanes), jnp.float32)
    nothing_c = jnp.zeros((rows // 2, lanes), jnp.float32)
    for c in range(3):
        for ref in (speed, field_a, field_b, relaxed):
            ref[c, 0] = nothing
            ref[c, depth + 1] = nothing
        for ref in (speed_c, delta):
            ref[c, 0] = nothing_c
            ref[c, half + 1] = nothing_c

    sides = 2 - first_t.astype(jnp.int32) - last_t.astype(jnp.int32)
    pl.semaphore_wait(barrier, slabs - 1 + slabs * sides)

    def slab_of(ref, g, width):
        return ref.at[:, pl.ds(1 + g * width, width)]

    def v_copy(g, slot):
        return pltpu.make_async_remote_copy(
            v_win.at[g, :, pl.ds(core_index * zsc, zsc)],
            speed.at[:, pl.ds(1 + slot * zs + core_index * zsc, zsc)],
            v_send.at[g], v_recv.at[slot],
            device_id=(t, g), device_id_type=MESH)

    def s_copy(slot, which):
        layers = speed.at[:, pl.ds(1 + slot * zs + which * zsc, zsc)]
        return pltpu.make_async_remote_copy(
            layers, layers, s_send.at[slot], s_recv.at[slot],
            device_id=(sibling, me), device_id_type=MESH)

    def c_copy(g, slot):
        return pltpu.make_async_remote_copy(
            c_win.at[g], slab_of(field_a, slot, zs), c_send.at[g], c_recv.at[slot],
            device_id=(t + 1, g), device_id_type=MESH)

    def w_copy(slot):
        return pltpu.make_async_remote_copy(
            slab_of(field_a, slot, zs), slab_of(relaxed, slot, zs), w_send.at[slot], w_recv.at[slot],
            device_id=(sibling, me), device_id_type=MESH)

    def r_copy(g, slot):
        return pltpu.make_async_remote_copy(
            slab_of(relaxed, g, zs), rel_slab.at[slot], r_send.at[g], r_recv.at[slot],
            device_id=(t, g), device_id_type=MESH)

    def d_copy(g, slot):
        return pltpu.make_async_remote_copy(
            slab_of(delta, g, zsc), delta_slab.at[slot], d_send.at[g], d_recv.at[slot],
            device_id=(t, g), device_id_type=MESH)

    def f_copy(z):
        return pltpu.make_async_remote_copy(
            sent.at[:, z], got.at[:, z], f_send.at[z], f_recv.at[z],
            device_id=(t + 1, me), device_id_type=MESH)

    for g in range(slabs):
        @pl.when(me != g)
        def _():
            v_copy(g, me).start()

    c_in.wait()
    cut(lambda c, z: c_ref[0, c, z], c_win)
    for g in range(slabs):
        @pl.when(jnp.logical_not(last_t))
        def _():
            c_copy(g, me).start()

        @pl.when(me == g)
        def _():
            speed[:, 1 + g * zs : 1 + (g + 1) * zs] = v_win[g]

    lane = lax.broadcasted_iota(jnp.int32, (rows, lanes), 1)
    even = lane % 2 == 0
    cell = lax.rem(lane + me * core - offset + y_all, y_all)

    def coefficients(vel, cf, n, ys):
        height = vel.shape[-2]
        row = lax.broadcasted_iota(jnp.int32, (height, lanes), 0)
        y = cell[:height]
        x_low = (row > 0).astype(jnp.float32)
        x_high = (row < height - 1).astype(jnp.float32)
        y_low = (y >= ys).astype(jnp.float32)
        y_high = (y < y_all - ys).astype(jnp.float32)

        def layer(z, carry):
            u = [vel[d, z + 1] for d in range(3)]
            low = [jnp.maximum(a, 0.0) + KAPPA for a in u]
            high = [KAPPA - jnp.minimum(a, 0.0) for a in u]
            cf[0, z] = low[0]
            cf[1, z] = high[0]
            cf[2, z] = low[1] * x_low
            cf[3, z] = high[1] * x_high
            cf[4, z] = low[2] * y_low
            cf[5, z] = high[2] * y_high
            centre = (1.0 - 6.0 * KAPPA) - (jnp.abs(u[0]) + jnp.abs(u[1]) + jnp.abs(u[2]))
            for c in range(3):
                grad = [
                    (vel[c, z + 2] - vel[c, z]) * 0.5,
                    (pltpu.roll(u[c], height - 1, 0) * x_high - pltpu.roll(u[c], 1, 0) * x_low) * 0.5,
                    (pltpu.roll(u[c], lanes - ys, 1) * y_high - pltpu.roll(u[c], ys, 1) * y_low) * 0.5,
                ]
                for d in range(3):
                    cf[6 + 3 * c + d, z] = grad[d] + centre if d == c else grad[d]
            return carry

        lax.fori_loop(0, n, layer, 0)

    def march_layer(src, put, cf, z, ys, extra=None):
        height = src.shape[-2]
        w = [src[c, z + 1] for c in range(3)]
        a = [cf[i, z] for i in range(6)]
        for c in range(3):
            new = cf[6 + 3 * c, z] * w[0] + cf[7 + 3 * c, z] * w[1] + cf[8 + 3 * c, z] * w[2]
            new = new + (a[0] * src[c, z] + a[1] * src[c, z + 2])
            new = new + (a[2] * pltpu.roll(w[c], 1, 0) + a[3] * pltpu.roll(w[c], height - 1, 0))
            new = new + (a[4] * pltpu.roll(w[c], ys, 1) + a[5] * pltpu.roll(w[c], lanes - ys, 1))
            put(c, new)

    def march(src, dst, n, unroll):
        def layers(block, carry):
            for k in range(unroll):
                z = block * unroll + k

                def put(c, new):
                    dst[c, z + 1] = new

                march_layer(src, put, cf, z, 1)
            return carry

        lax.fori_loop(0, n // unroll, layers, 0)

    def restrict(src, dst, scale):
        def layer(z, carry):
            for c in range(3):
                both = src[c, 2 * z + 1] + src[c, 2 * z + 2]
                both = both + jnp.where(even, pltpu.roll(both, lanes - 1, 1), pltpu.roll(both, 1, 1))
                for part in range(lanes // LANES):
                    at = slice(part * LANES, (part + 1) * LANES)
                    pairs[part, c, z] = both[:, at]
            for c in range(3):
                for part in range(lanes // LANES):
                    at = slice(part * LANES, (part + 1) * LANES)
                    dst[c, z + 1, :, at] = scale * (
                        pairs[part, c, z, pl.ds(0, rows // 2, stride=2), :]
                        + pairs[part, c, z, pl.ds(1, rows // 2, stride=2), :])
            return carry

        lax.fori_loop(0, half, layer, 0)

    for g in range(slabs):
        @pl.when(me != g)
        def _():
            v_copy(g, g).wait_recv()
            s_copy(g, core_index).start()

    for g in range(slabs):
        @pl.when(me != g)
        def _():
            s_copy(g, 1 - core_index).wait_recv()

    coefficients(speed, cf, depth, 1)
    restrict(speed, speed_c, 0.25)
    coefficients(speed_c, cf_c, half, 2)

    @pl.when(first_t)
    def _():
        for g in range(slabs):
            w_copy(g).wait_recv()

    @pl.when(jnp.logical_not(first_t))
    def _():
        for g in range(slabs):
            c_copy(g, g).wait_recv()

            @pl.when(t == 1)
            def _():
                w_copy(g).start()

        march(field_a, field_b, depth, 2)

        @pl.when(t == 1)
        def _():
            for g in range(slabs):
                w_copy(g).wait_send()

        march(field_b, field_a, depth, 2)
        march(field_a, field_b, depth, 2)
        march(field_b, relaxed, depth, 2)

    for g in range(slabs):
        @pl.when(me != g)
        def _():
            r_copy(g, me).start()

        @pl.when(me == g)
        def _():
            rel_slab[g] = relaxed[:, 1 + g * zs : 1 + (g + 1) * zs]

    march(relaxed, field_b, depth, 2)
    march(field_b, field_a, depth, 2)
    march(field_a, field_b, depth, 2)
    march(field_b, field_a, depth, 2)
    restrict(field_a, r_again, 0.125)
    restrict(relaxed, r_relaxed, 0.125)

    @pl.when(first_t)
    def _():
        delta[:, 1 : half + 1] = jnp.zeros((3, half, rows // 2, lanes), jnp.float32)

    def send_on(z):
        @pl.when(jnp.logical_not(last_t))
        def _():
            def put(c, new):
                sent[c, z] = new + r_again[c, z + 1]

            march_layer(delta, put, cf_c, z, 2)
            f_copy(z).start()

    for z in range(half):
        @pl.when(jnp.logical_not(first_t))
        def _():
            f_copy(z).wait_recv()
            delta[:, z + 1] = got[:, z] - r_relaxed[:, z + 1]

        if z > 0:
            send_on(z - 1)
        if z % zsc == zsc - 1:
            g = z // zsc

            @pl.when(me != g)
            def _():
                d_copy(g, me).start()

            @pl.when(me == g)
            def _():
                delta_slab[g] = delta[:, 1 + g * zsc : 1 + (g + 1) * zsc]
    send_on(half - 1)

    tile_lane = lax.broadcasted_iota(jnp.int32, (rows, LANES), 1)

    def joined(read, tile):
        total = None
        for g in range(slabs):
            start = g * core - tile * LANES
            if start < 0 or start >= LANES:
                continue
            shift = (start - offset) % lanes
            piece = read(g)
            piece = pltpu.roll(piece, shift, 1) if shift else piece
            piece = piece[:, :LANES]
            total = piece if total is None else jnp.where(tile_lane[: piece.shape[0]] >= start, piece, total)
        return total

    for g in range(slabs):
        @pl.when(me != g)
        def _():
            r_copy(g, g).wait_recv()

    def rel_layer(z, carry):
        for c in range(3):
            for tile in range(y_all // LANES):
                out_ref[0, c, z, :, tile * LANES : (tile + 1) * LANES] = joined(lambda g: rel_slab[g, c, z], tile)
        return carry

    lax.fori_loop(0, zs, rel_layer, 0)

    for g in range(slabs):
        @pl.when(me != g)
        def _():
            d_copy(g, g).wait_recv()

    def out_layer(z, carry):
        for c in range(3):
            for tile in range(y_all // LANES):
                at = slice(tile * LANES, (tile + 1) * LANES)
                coarse = joined(lambda g: delta_slab[g, c, z], tile)
                fine_tmp[tile, c, z, pl.ds(0, rows // 2, stride=2), :] = coarse
                fine_tmp[tile, c, z, pl.ds(1, rows // 2, stride=2), :] = coarse
            for tile in range(y_all // LANES):
                at = slice(tile * LANES, (tile + 1) * LANES)
                fine = fine_tmp[tile, c, z]
                for k in range(2):
                    out_ref[0, c, 2 * z + k, :, at] = out_ref[0, c, 2 * z + k, :, at] + fine
        return carry

    lax.fori_loop(0, zsc, out_layer, 0)

    for g in range(slabs):
        @pl.when(me != g)
        def _():
            v_copy(g, me).wait_send()
            s_copy(g, core_index).wait_send()
            r_copy(g, me).wait_send()
            d_copy(g, me).wait_send()

        @pl.when(jnp.logical_not(last_t))
        def _():
            c_copy(g, me).wait_send()

    @pl.when(jnp.logical_not(last_t))
    def _():
        for z in range(half):
            f_copy(z).wait_send()


def local(c_states, velocity):
    intervals = lax.axis_size("tm")
    slabs = lax.axis_size("gz")
    zs, rows, y_all = velocity.shape[1:]
    core = y_all // slabs
    depth = zs * slabs
    half = depth // 2
    halo = 2 * STEPS + 2 * (intervals - 1)
    lanes = min(y_all, -(-(core + 2 * halo) // LANES) * LANES)
    offset = (lanes - core) // 4 * 2
    f32 = jnp.float32
    windows = pltpu.VMEM((slabs, 3, zs, rows, lanes), f32)
    field = pltpu.VMEM((3, depth + 2, rows, lanes), f32)
    coarse = pltpu.VMEM((3, half + 2, rows // 2, lanes), f32)
    flat = pltpu.VMEM((3, half, rows // 2, lanes), f32)
    layered = pltpu.SemaphoreType.DMA((half,))
    several = pltpu.SemaphoreType.DMA((slabs,))
    return pl.pallas_call(
        functools.partial(kernel, intervals, slabs, offset),
        out_shape=jax.ShapeDtypeStruct(c_states.shape, f32),
        in_specs=[pl.BlockSpec(memory_space=pl.ANY)] * 2,
        out_specs=pl.BlockSpec(memory_space=pltpu.VMEM),
        scratch_shapes=[
            pltpu.VMEM(c_states.shape, f32),
            pltpu.VMEM(velocity.shape, f32),
            windows, windows, field, field, field, field,
            pltpu.VMEM((15, depth, rows, lanes), f32),
            coarse,
            pltpu.VMEM((15, half, rows // 2, lanes), f32),
            pltpu.VMEM((lanes // LANES, 3, half, rows, LANES), f32),
            coarse, coarse, coarse, flat, flat,
            windows,
            pltpu.VMEM((slabs, 3, zs // 2, rows // 2, lanes), f32),
            pltpu.VMEM((y_all // LANES, 3, zs // 2, rows, LANES), f32),
            pltpu.SemaphoreType.DMA((2,)),
            several, several, several, several, several, several, several, several,
            several, several, several, several,
            layered, layered,
        ],
        compiler_params=pltpu.CompilerParams(
            collective_id=0, has_side_effects=True, vmem_limit_bytes=56 * 2**20
        ),
    )(c_states, velocity)


def solution(mesh):
    return jax.shard_map(
        local,
        mesh=mesh,
        in_specs=(P("tm", None, "gz", None, None), P(None, "gz", None, None)),
        out_specs=P("tm", None, "gz", None, None),
        check_vma=False,
    )
```

```python
import functools

import jax
import jax.numpy as jnp
from jax import lax
from jax.experimental import pallas as pl
from jax.experimental.pallas import tpu as pltpu
from jax.sharding import PartitionSpec as P

STEPS = 4
KAPPA = 0.04
LANES = 128
MESH = pl.DeviceIdType.MESH


def loop(n, body, most):
    width = max(d for d in range(1, max(most, 1) + 1) if n % d == 0)

    def block(first):
        lax.fori_loop(0, width, lambda k, carry: (body(first + k), carry)[1], 0, unroll=True)

    if width == n:
        block(0)
    else:
        lax.fori_loop(0, n // width, lambda b, carry: (block(b * width), carry)[1], 0)


def kernel(
    intervals, slabs, offset,
    c_hbm, v_hbm, out_ref,
    c_ref, v_ref, v_win, c_win, speed, field_a, field_b, relaxed, cf, speed_c, cf_c,
    pairs, r_relaxed, r_again, delta, sent, got, rel_slab, delta_slab, fine_tmp,
    in_sem, v_send, v_recv, s_send, s_recv, c_send, c_recv, w_send, w_recv, r_send, r_recv, d_send, d_recv, f_send, f_recv,
):
    t = lax.axis_index("tm")
    me = lax.axis_index("gz")
    first_t = t == 0
    last_t = t == intervals - 1
    zs, rows, y_all = v_ref.shape[1:]
    core = y_all // slabs
    depth = zs * slabs
    half = depth // 2
    zsc = zs // 2
    lanes = v_win.shape[-1]
    wide = 8 * LANES // lanes

    v_in = pltpu.make_async_copy(v_hbm, v_ref, in_sem.at[0])
    c_in = pltpu.make_async_copy(c_hbm, c_ref, in_sem.at[1])
    v_in.start()
    c_in.start()
    core_index = t % 2
    sibling = t + 1 - 2 * core_index

    barrier = pltpu.get_barrier_semaphore()
    for g in range(slabs):
        @pl.when(me != g)
        def _():
            pl.semaphore_signal(barrier, inc=1, device_id=(t, g), device_id_type=MESH)

        @pl.when(jnp.logical_not(first_t))
        def _():
            pl.semaphore_signal(barrier, inc=1, device_id=(t - 1, g), device_id_type=MESH)

        @pl.when(jnp.logical_not(last_t))
        def _():
            pl.semaphore_signal(barrier, inc=1, device_id=(t + 1, g), device_id_type=MESH)

    def cut(read, target):
        def layer(z):
            for c in range(3):
                whole = read(c, z)
                for g in range(slabs):
                    shift = (offset - g * core) % y_all
                    turned = pltpu.roll(whole, shift, 1) if shift else whole
                    target[g, c, z] = turned[:, :lanes]

        loop(zs, layer, 16 // slabs)

    v_in.wait()
    cut(lambda c, z: v_ref[c, z], v_win)
    nothing = jnp.zeros((rows, lanes), jnp.float32)
    nothing_c = jnp.zeros((rows // 2, lanes), jnp.float32)
    for c in range(3):
        for ref in (speed, field_a, field_b, relaxed):
            ref[c, 0] = nothing
            ref[c, depth + 1] = nothing
        for ref in (speed_c, delta):
            ref[c, 0] = nothing_c
            ref[c, half + 1] = nothing_c

    sides = 2 - first_t.astype(jnp.int32) - last_t.astype(jnp.int32)
    pl.semaphore_wait(barrier, slabs - 1 + slabs * sides)

    def slab_of(ref, g, width):
        return ref.at[:, pl.ds(1 + g * width, width)]

    def v_copy(g, slot):
        return pltpu.make_async_remote_copy(
            v_win.at[g, :, pl.ds(core_index * zsc, zsc)],
            speed.at[:, pl.ds(1 + slot * zs + core_index * zsc, zsc)],
            v_send.at[g], v_recv.at[slot],
            device_id=(t, g), device_id_type=MESH)

    def s_copy(slot, which):
        layers = speed.at[:, pl.ds(1 + slot * zs + which * zsc, zsc)]
        return pltpu.make_async_remote_copy(
            layers, layers, s_send.at[slot], s_recv.at[slot],
            device_id=(sibling, me), device_id_type=MESH)

    def c_copy(g, slot):
        return pltpu.make_async_remote_copy(
            c_win.at[g], slab_of(field_a, slot, zs), c_send.at[g], c_recv.at[slot],
            device_id=(t + 1, g), device_id_type=MESH)

    def w_copy(slot):
        return pltpu.make_async_remote_copy(
            slab_of(field_a, slot, zs), slab_of(relaxed, slot, zs), w_send.at[slot], w_recv.at[slot],
            device_id=(sibling, me), device_id_type=MESH)

    def r_copy(g, slot):
        return pltpu.make_async_remote_copy(
            slab_of(relaxed, g, zs), rel_slab.at[slot], r_send.at[g], r_recv.at[slot],
            device_id=(t, g), device_id_type=MESH)

    def d_copy(g, slot):
        return pltpu.make_async_remote_copy(
            slab_of(delta, g, zsc), delta_slab.at[slot], d_send.at[g], d_recv.at[slot],
            device_id=(t, g), device_id_type=MESH)

    def f_copy(z):
        return pltpu.make_async_remote_copy(
            sent.at[:, z], got.at[:, z], f_send.at[z], f_recv.at[z],
            device_id=(t + 1, me), device_id_type=MESH)

    for g in range(slabs):
        @pl.when(me != g)
        def _():
            v_copy(g, me).start()

    c_in.wait()
    cut(lambda c, z: c_ref[0, c, z], c_win)
    for g in range(slabs):
        @pl.when(jnp.logical_not(last_t))
        def _():
            c_copy(g, me).start()

        @pl.when(me == g)
        def _():
            speed[:, 1 + g * zs : 1 + (g + 1) * zs] = v_win[g]

    lane = lax.broadcasted_iota(jnp.int32, (rows, lanes), 1)
    even = lane % 2 == 0
    cell = lax.rem(lane + me * core - offset + y_all, y_all)

    def coefficients(vel, cf, n, ys):
        height = vel.shape[-2]
        row = lax.broadcasted_iota(jnp.int32, (height, lanes), 0)
        y = cell[:height]
        x_low = (row > 0).astype(jnp.float32)
        x_high = (row < height - 1).astype(jnp.float32)
        y_low = (y >= ys).astype(jnp.float32)
        y_high = (y < y_all - ys).astype(jnp.float32)

        def layer(z):
            u = [vel[d, z + 1] for d in range(3)]
            low = [jnp.maximum(a, 0.0) + KAPPA for a in u]
            high = [KAPPA - jnp.minimum(a, 0.0) for a in u]
            cf[0, z] = low[0]
            cf[1, z] = high[0]
            cf[2, z] = low[1] * x_low
            cf[3, z] = high[1] * x_high
            cf[4, z] = low[2] * y_low
            cf[5, z] = high[2] * y_high
            centre = (1.0 - 6.0 * KAPPA) - (jnp.abs(u[0]) + jnp.abs(u[1]) + jnp.abs(u[2]))
            for c in range(3):
                grad = [
                    (vel[c, z + 2] - vel[c, z]) * 0.5,
                    (pltpu.roll(u[c], height - 1, 0) * x_high - pltpu.roll(u[c], 1, 0) * x_low) * 0.5,
                    (pltpu.roll(u[c], lanes - ys, 1) * y_high - pltpu.roll(u[c], ys, 1) * y_low) * 0.5,
                ]
                for d in range(3):
                    cf[6 + 3 * c + d, z] = grad[d] + centre if d == c else grad[d]

        loop(n, layer, wide)

    def march_layer(src, put, cf, z, ys, extra=None):
        height = src.shape[-2]
        w = [src[c, z + 1] for c in range(3)]
        a = [cf[i, z] for i in range(6)]
        for c in range(3):
            new = cf[6 + 3 * c, z] * w[0] + cf[7 + 3 * c, z] * w[1] + cf[8 + 3 * c, z] * w[2]
            new = new + (a[0] * src[c, z] + a[1] * src[c, z + 2])
            new = new + (a[2] * pltpu.roll(w[c], 1, 0) + a[3] * pltpu.roll(w[c], height - 1, 0))
            new = new + (a[4] * pltpu.roll(w[c], ys, 1) + a[5] * pltpu.roll(w[c], lanes - ys, 1))
            put(c, new)

    def march(src, dst, n, unroll):
        def layer(z):
            def put(c, new):
                dst[c, z + 1] = new

            march_layer(src, put, cf, z, 1)

        loop(n, layer, unroll)

    def restrict(src, dst, scale):
        def layer(z):
            for c in range(3):
                both = src[c, 2 * z + 1] + src[c, 2 * z + 2]
                both = both + jnp.where(even, pltpu.roll(both, lanes - 1, 1), pltpu.roll(both, 1, 1))
                for part in range(lanes // LANES):
                    at = slice(part * LANES, (part + 1) * LANES)
                    pairs[part, c, z] = both[:, at]
            for c in range(3):
                for part in range(lanes // LANES):
                    at = slice(part * LANES, (part + 1) * LANES)
                    dst[c, z + 1, :, at] = scale * (
                        pairs[part, c, z, pl.ds(0, rows // 2, stride=2), :]
                        + pairs[part, c, z, pl.ds(1, rows // 2, stride=2), :])

        loop(half, layer, wide)

    for g in range(slabs):
        @pl.when(me != g)
        def _():
            v_copy(g, g).wait_recv()
            s_copy(g, core_index).start()

    for g in range(slabs):
        @pl.when(me != g)
        def _():
            s_copy(g, 1 - core_index).wait_recv()

    coefficients(speed, cf, depth, 1)
    restrict(speed, speed_c, 0.25)
    coefficients(speed_c, cf_c, half, 2)

    @pl.when(first_t)
    def _():
        for g in range(slabs):
            w_copy(g).wait_recv()

    @pl.when(jnp.logical_not(first_t))
    def _():
        for g in range(slabs):
            c_copy(g, g).wait_recv()

            @pl.when(t == 1)
            def _():
                w_copy(g).start()

        march(field_a, field_b, depth, wide)

        @pl.when(t == 1)
        def _():
            for g in range(slabs):
                w_copy(g).wait_send()

        march(field_b, field_a, depth, wide)
        march(field_a, field_b, depth, wide)
        march(field_b, relaxed, depth, wide)

    for g in range(slabs):
        @pl.when(me != g)
        def _():
            r_copy(g, me).start()

        @pl.when(me == g)
        def _():
            rel_slab[g] = relaxed[:, 1 + g * zs : 1 + (g + 1) * zs]

    march(relaxed, field_b, depth, wide)
    march(field_b, field_a, depth, wide)
    march(field_a, field_b, depth, wide)
    march(field_b, field_a, depth, wide)
    restrict(field_a, r_again, 0.125)
    restrict(relaxed, r_relaxed, 0.125)

    @pl.when(first_t)
    def _():
        delta[:, 1 : half + 1] = jnp.zeros((3, half, rows // 2, lanes), jnp.float32)

    def send_on(z):
        @pl.when(jnp.logical_not(last_t))
        def _():
            def put(c, new):
                sent[c, z] = new + r_again[c, z + 1]

            march_layer(delta, put, cf_c, z, 2)
            f_copy(z).start()

    for z in range(half):
        @pl.when(jnp.logical_not(first_t))
        def _():
            f_copy(z).wait_recv()
            delta[:, z + 1] = got[:, z] - r_relaxed[:, z + 1]

        if z > 0:
            send_on(z - 1)
        if z % zsc == zsc - 1:
            g = z // zsc

            @pl.when(me != g)
            def _():
                d_copy(g, me).start()

            @pl.when(me == g)
            def _():
                delta_slab[g] = delta[:, 1 + g * zsc : 1 + (g + 1) * zsc]
    send_on(half - 1)

    tile_lane = lax.broadcasted_iota(jnp.int32, (rows, LANES), 1)

    def joined(read, tile):
        total = None
        for g in range(slabs):
            start = g * core - tile * LANES
            if start < 0 or start >= LANES:
                continue
            shift = (start - offset) % lanes
            piece = read(g)
            piece = pltpu.roll(piece, shift, 1) if shift else piece
            piece = piece[:, :LANES]
            total = piece if total is None else jnp.where(tile_lane[: piece.shape[0]] >= start, piece, total)
        return total

    for g in range(slabs):
        @pl.when(me != g)
        def _():
            r_copy(g, g).wait_recv()

    def rel_layer(z):
        for c in range(3):
            for tile in range(y_all // LANES):
                out_ref[0, c, z, :, tile * LANES : (tile + 1) * LANES] = joined(lambda g: rel_slab[g, c, z], tile)

    loop(zs, rel_layer, zs)

    for g in range(slabs):
        @pl.when(me != g)
        def _():
            d_copy(g, g).wait_recv()

    def out_layer(z):
        for c in range(3):
            for tile in range(y_all // LANES):
                at = slice(tile * LANES, (tile + 1) * LANES)
                coarse = joined(lambda g: delta_slab[g, c, z], tile)
                fine_tmp[tile, c, z, pl.ds(0, rows // 2, stride=2), :] = coarse
                fine_tmp[tile, c, z, pl.ds(1, rows // 2, stride=2), :] = coarse
            for tile in range(y_all // LANES):
                at = slice(tile * LANES, (tile + 1) * LANES)
                fine = fine_tmp[tile, c, z]
                for k in range(2):
                    out_ref[0, c, 2 * z + k, :, at] = out_ref[0, c, 2 * z + k, :, at] + fine

    loop(zsc, out_layer, zsc)

    for g in range(slabs):
        @pl.when(me != g)
        def _():
            v_copy(g, me).wait_send()
            s_copy(g, core_index).wait_send()
            r_copy(g, me).wait_send()
            d_copy(g, me).wait_send()

        @pl.when(jnp.logical_not(last_t))
        def _():
            c_copy(g, me).wait_send()

    @pl.when(jnp.logical_not(last_t))
    def _():
        for z in range(half):
            f_copy(z).wait_send()


def local(c_states, velocity):
    intervals = lax.axis_size("tm")
    slabs = lax.axis_size("gz")
    zs, rows, y_all = velocity.shape[1:]
    core = y_all // slabs
    depth = zs * slabs
    half = depth // 2
    halo = 2 * STEPS + 2 * (intervals - 1)
    lanes = min(y_all, -(-(core + 2 * halo) // LANES) * LANES)
    offset = (lanes - core) // 4 * 2
    f32 = jnp.float32
    windows = pltpu.VMEM((slabs, 3, zs, rows, lanes), f32)
    field = pltpu.VMEM((3, depth + 2, rows, lanes), f32)
    coarse = pltpu.VMEM((3, half + 2, rows // 2, lanes), f32)
    flat = pltpu.VMEM((3, half, rows // 2, lanes), f32)
    layered = pltpu.SemaphoreType.DMA((half,))
    several = pltpu.SemaphoreType.DMA((slabs,))
    return pl.pallas_call(
        functools.partial(kernel, intervals, slabs, offset),
        out_shape=jax.ShapeDtypeStruct(c_states.shape, f32),
        in_specs=[pl.BlockSpec(memory_space=pl.ANY)] * 2,
        out_specs=pl.BlockSpec(memory_space=pltpu.VMEM),
        scratch_shapes=[
            pltpu.VMEM(c_states.shape, f32),
            pltpu.VMEM(velocity.shape, f32),
            windows, windows, field, field, field, field,
            pltpu.VMEM((15, depth, rows, lanes), f32),
            coarse,
            pltpu.VMEM((15, half, rows // 2, lanes), f32),
            pltpu.VMEM((lanes // LANES, 3, half, rows, LANES), f32),
            coarse, coarse, coarse, flat, flat,
            windows,
            pltpu.VMEM((slabs, 3, zs // 2, rows // 2, lanes), f32),
            pltpu.VMEM((y_all // LANES, 3, zs // 2, rows, LANES), f32),
            pltpu.SemaphoreType.DMA((2,)),
            several, several, several, several, several, several, several, several,
            several, several, several, several,
            layered, layered,
        ],
        compiler_params=pltpu.CompilerParams(
            collective_id=0, has_side_effects=True, vmem_limit_bytes=56 * 2**20
        ),
    )(c_states, velocity)


def solution(mesh):
    return jax.shard_map(
        local,
        mesh=mesh,
        in_specs=(P("tm", None, "gz", None, None), P(None, "gz", None, None)),
        out_specs=P("tm", None, "gz", None, None),
        check_vma=False,
    )
```

```python
import functools

import jax
import jax.numpy as jnp
from jax import lax
from jax.experimental import pallas as pl
from jax.experimental.pallas import tpu as pltpu
from jax.sharding import PartitionSpec as P

STEPS = 4
KAPPA = 0.04
LANES = 128
MESH = pl.DeviceIdType.MESH


def loop(n, body, most):
    width = max(d for d in range(1, max(most, 1) + 1) if n % d == 0)

    def block(first):
        lax.fori_loop(0, width, lambda k, carry: (body(first + k), carry)[1], 0, unroll=True)

    if width == n:
        block(0)
    else:
        lax.fori_loop(0, n // width, lambda b, carry: (block(b * width), carry)[1], 0)


def kernel(
    intervals, slabs, offset,
    c_hbm, v_hbm, out_ref,
    c_ref, v_ref, v_win, c_win, speed, field_a, field_b, relaxed, cf, speed_c, cf_c,
    pairs, r_relaxed, r_again, delta, sent, got, rel_slab, delta_slab, fine_tmp,
    in_sem, v_send, v_recv, s_send, s_recv, c_send, c_recv, w_send, w_recv, r_send, r_recv, d_send, d_recv, f_send, f_recv,
):
    t = lax.axis_index("tm")
    me = lax.axis_index("gz")
    first_t = t == 0
    last_t = t == intervals - 1
    zs, rows, y_all = v_ref.shape[1:]
    core = y_all // slabs
    depth = zs * slabs
    half = depth // 2
    zsc = zs // 2
    lanes = v_win.shape[-1]
    wide = 16 * LANES // lanes

    v_in = pltpu.make_async_copy(v_hbm, v_ref, in_sem.at[0])
    c_in = pltpu.make_async_copy(c_hbm, c_ref, in_sem.at[1])
    v_in.start()
    c_in.start()
    core_index = t % 2
    sibling = t + 1 - 2 * core_index

    barrier = pltpu.get_barrier_semaphore()
    for g in range(slabs):
        @pl.when(me != g)
        def _():
            pl.semaphore_signal(barrier, inc=1, device_id=(t, g), device_id_type=MESH)

        @pl.when(jnp.logical_not(first_t))
        def _():
            pl.semaphore_signal(barrier, inc=1, device_id=(t - 1, g), device_id_type=MESH)

        @pl.when(jnp.logical_not(last_t))
        def _():
            pl.semaphore_signal(barrier, inc=1, device_id=(t + 1, g), device_id_type=MESH)

    def cut(read, target):
        def layer(z):
            for c in range(3):
                whole = read(c, z)
                for g in range(slabs):
                    shift = (offset - g * core) % y_all
                    turned = pltpu.roll(whole, shift, 1) if shift else whole
                    target[g, c, z] = turned[:, :lanes]

        loop(zs, layer, 16 // slabs)

    v_in.wait()
    cut(lambda c, z: v_ref[c, z], v_win)
    nothing = jnp.zeros((rows, lanes), jnp.float32)
    nothing_c = jnp.zeros((rows // 2, lanes), jnp.float32)
    for c in range(3):
        for ref in (speed, field_a, field_b, relaxed):
            ref[c, 0] = nothing
            ref[c, depth + 1] = nothing
        for ref in (speed_c, delta):
            ref[c, 0] = nothing_c
            ref[c, half + 1] = nothing_c

    sides = 2 - first_t.astype(jnp.int32) - last_t.astype(jnp.int32)
    pl.semaphore_wait(barrier, slabs - 1 + slabs * sides)

    def slab_of(ref, g, width):
        return ref.at[:, pl.ds(1 + g * width, width)]

    def v_copy(g, slot):
        return pltpu.make_async_remote_copy(
            v_win.at[g, :, pl.ds(core_index * zsc, zsc)],
            speed.at[:, pl.ds(1 + slot * zs + core_index * zsc, zsc)],
            v_send.at[g], v_recv.at[slot],
            device_id=(t, g), device_id_type=MESH)

    def s_copy(slot, which):
        layers = speed.at[:, pl.ds(1 + slot * zs + which * zsc, zsc)]
        return pltpu.make_async_remote_copy(
            layers, layers, s_send.at[slot], s_recv.at[slot],
            device_id=(sibling, me), device_id_type=MESH)

    def c_copy(g, slot):
        return pltpu.make_async_remote_copy(
            c_win.at[g], slab_of(field_a, slot, zs), c_send.at[g], c_recv.at[slot],
            device_id=(t + 1, g), device_id_type=MESH)

    def w_copy(slot):
        return pltpu.make_async_remote_copy(
            slab_of(field_a, slot, zs), slab_of(relaxed, slot, zs), w_send.at[slot], w_recv.at[slot],
            device_id=(sibling, me), device_id_type=MESH)

    def r_copy(g, slot):
        return pltpu.make_async_remote_copy(
            slab_of(relaxed, g, zs), rel_slab.at[slot], r_send.at[g], r_recv.at[slot],
            device_id=(t, g), device_id_type=MESH)

    def d_copy(g, slot):
        return pltpu.make_async_remote_copy(
            slab_of(delta, g, zsc), delta_slab.at[slot], d_send.at[g], d_recv.at[slot],
            device_id=(t, g), device_id_type=MESH)

    def f_copy(z):
        return pltpu.make_async_remote_copy(
            sent.at[z], got.at[z], f_send.at[z], f_recv.at[z],
            device_id=(t + 1, me), device_id_type=MESH)

    for g in range(slabs):
        @pl.when(me != g)
        def _():
            v_copy(g, me).start()

    c_in.wait()
    cut(lambda c, z: c_ref[0, c, z], c_win)
    for g in range(slabs):
        @pl.when(jnp.logical_not(last_t))
        def _():
            c_copy(g, me).start()

        @pl.when(me == g)
        def _():
            speed[:, 1 + g * zs : 1 + (g + 1) * zs] = v_win[g]

    lane = lax.broadcasted_iota(jnp.int32, (rows, lanes), 1)
    even = lane % 2 == 0
    cell = lax.rem(lane + me * core - offset + y_all, y_all)

    def coefficients(vel, cf, n, ys):
        height = vel.shape[-2]
        row = lax.broadcasted_iota(jnp.int32, (height, lanes), 0)
        y = cell[:height]
        x_low = (row > 0).astype(jnp.float32)
        x_high = (row < height - 1).astype(jnp.float32)
        y_low = (y >= ys).astype(jnp.float32)
        y_high = (y < y_all - ys).astype(jnp.float32)

        def layer(z):
            u = [vel[d, z + 1] for d in range(3)]
            low = [jnp.maximum(a, 0.0) + KAPPA for a in u]
            high = [KAPPA - jnp.minimum(a, 0.0) for a in u]
            cf[0, z] = low[0]
            cf[1, z] = high[0]
            cf[2, z] = low[1] * x_low
            cf[3, z] = high[1] * x_high
            cf[4, z] = low[2] * y_low
            cf[5, z] = high[2] * y_high
            centre = (1.0 - 6.0 * KAPPA) - (jnp.abs(u[0]) + jnp.abs(u[1]) + jnp.abs(u[2]))
            for c in range(3):
                grad = [
                    (vel[c, z + 2] - vel[c, z]) * 0.5,
                    (pltpu.roll(u[c], height - 1, 0) * x_high - pltpu.roll(u[c], 1, 0) * x_low) * 0.5,
                    (pltpu.roll(u[c], lanes - ys, 1) * y_high - pltpu.roll(u[c], ys, 1) * y_low) * 0.5,
                ]
                for d in range(3):
                    cf[6 + 3 * c + d, z] = grad[d] + centre if d == c else grad[d]

        loop(n, layer, wide)

    def march_layer(src, put, cf, z, ys, extra=None):
        height = src.shape[-2]
        w = [src[c, z + 1] for c in range(3)]
        a = [cf[i, z] for i in range(6)]
        for c in range(3):
            new = cf[6 + 3 * c, z] * w[0] + cf[7 + 3 * c, z] * w[1] + cf[8 + 3 * c, z] * w[2]
            new = new + (a[0] * src[c, z] + a[1] * src[c, z + 2])
            new = new + (a[2] * pltpu.roll(w[c], 1, 0) + a[3] * pltpu.roll(w[c], height - 1, 0))
            new = new + (a[4] * pltpu.roll(w[c], ys, 1) + a[5] * pltpu.roll(w[c], lanes - ys, 1))
            put(c, new)

    def march(src, dst, n, unroll):
        def layer(z):
            def put(c, new):
                dst[c, z + 1] = new

            march_layer(src, put, cf, z, 1)

        loop(n, layer, unroll)

    def restrict(src, dst, scale):
        def layer(z):
            for c in range(3):
                both = src[c, 2 * z + 1] + src[c, 2 * z + 2]
                both = both + jnp.where(even, pltpu.roll(both, lanes - 1, 1), pltpu.roll(both, 1, 1))
                for part in range(lanes // LANES):
                    at = slice(part * LANES, (part + 1) * LANES)
                    pairs[part, c, z] = both[:, at]
            for c in range(3):
                for part in range(lanes // LANES):
                    at = slice(part * LANES, (part + 1) * LANES)
                    dst[c, z + 1, :, at] = scale * (
                        pairs[part, c, z, pl.ds(0, rows // 2, stride=2), :]
                        + pairs[part, c, z, pl.ds(1, rows // 2, stride=2), :])

        loop(half, layer, wide)

    for g in range(slabs):
        @pl.when(me != g)
        def _():
            v_copy(g, g).wait_recv()
            s_copy(g, core_index).start()

    for g in range(slabs):
        @pl.when(me != g)
        def _():
            s_copy(g, 1 - core_index).wait_recv()

    coefficients(speed, cf, depth, 1)
    restrict(speed, speed_c, 0.25)
    coefficients(speed_c, cf_c, half, 2)

    @pl.when(first_t)
    def _():
        for g in range(slabs):
            w_copy(g).wait_recv()

    @pl.when(jnp.logical_not(first_t))
    def _():
        for g in range(slabs):
            c_copy(g, g).wait_recv()

            @pl.when(t == 1)
            def _():
                w_copy(g).start()

        march(field_a, field_b, depth, wide)

        @pl.when(t == 1)
        def _():
            for g in range(slabs):
                w_copy(g).wait_send()

        march(field_b, field_a, depth, wide)
        march(field_a, field_b, depth, wide)
        march(field_b, relaxed, depth, wide)

    for g in range(slabs):
        @pl.when(me != g)
        def _():
            r_copy(g, me).start()

        @pl.when(me == g)
        def _():
            rel_slab[g] = relaxed[:, 1 + g * zs : 1 + (g + 1) * zs]

    march(relaxed, field_b, depth, wide)
    march(field_b, field_a, depth, wide)
    march(field_a, field_b, depth, wide)
    march(field_b, field_a, depth, wide)
    restrict(field_a, r_again, 0.125)
    restrict(relaxed, r_relaxed, 0.125)

    @pl.when(first_t)
    def _():
        delta[:, 1 : half + 1] = jnp.zeros((3, half, rows // 2, lanes), jnp.float32)

    def send_on(z):
        @pl.when(jnp.logical_not(last_t))
        def _():
            def put(c, new):
                sent[z, c] = new + r_again[c, z + 1]

            march_layer(delta, put, cf_c, z, 2)
            f_copy(z).start()

    for z in range(half):
        @pl.when(jnp.logical_not(first_t))
        def _():
            f_copy(z).wait_recv()
            delta[:, z + 1] = got[z] - r_relaxed[:, z + 1]

        if z > 0:
            send_on(z - 1)
        if z % zsc == zsc - 1:
            g = z // zsc

            @pl.when(me != g)
            def _():
                d_copy(g, me).start()

            @pl.when(me == g)
            def _():
                delta_slab[g] = delta[:, 1 + g * zsc : 1 + (g + 1) * zsc]
    send_on(half - 1)

    tile_lane = lax.broadcasted_iota(jnp.int32, (rows, LANES), 1)

    def joined(read, tile):
        total = None
        for g in range(slabs):
            start = g * core - tile * LANES
            if start < 0 or start >= LANES:
                continue
            shift = (start - offset) % lanes
            piece = read(g)
            piece = pltpu.roll(piece, shift, 1) if shift else piece
            piece = piece[:, :LANES]
            total = piece if total is None else jnp.where(tile_lane[: piece.shape[0]] >= start, piece, total)
        return total

    for g in range(slabs):
        @pl.when(me != g)
        def _():
            r_copy(g, g).wait_recv()

    def rel_layer(z):
        for c in range(3):
            for tile in range(y_all // LANES):
                out_ref[0, c, z, :, tile * LANES : (tile + 1) * LANES] = joined(lambda g: rel_slab[g, c, z], tile)

    loop(zs, rel_layer, zs)

    for g in range(slabs):
        @pl.when(me != g)
        def _():
            d_copy(g, g).wait_recv()

    def out_layer(z):
        for c in range(3):
            for tile in range(y_all // LANES):
                at = slice(tile * LANES, (tile + 1) * LANES)
                coarse = joined(lambda g: delta_slab[g, c, z], tile)
                fine_tmp[tile, c, z, pl.ds(0, rows // 2, stride=2), :] = coarse
                fine_tmp[tile, c, z, pl.ds(1, rows // 2, stride=2), :] = coarse
            for tile in range(y_all // LANES):
                at = slice(tile * LANES, (tile + 1) * LANES)
                fine = fine_tmp[tile, c, z]
                for k in range(2):
                    out_ref[0, c, 2 * z + k, :, at] = out_ref[0, c, 2 * z + k, :, at] + fine

    loop(zsc, out_layer, zsc)

    for g in range(slabs):
        @pl.when(me != g)
        def _():
            v_copy(g, me).wait_send()
            s_copy(g, core_index).wait_send()
            r_copy(g, me).wait_send()
            d_copy(g, me).wait_send()

        @pl.when(jnp.logical_not(last_t))
        def _():
            c_copy(g, me).wait_send()

    @pl.when(jnp.logical_not(last_t))
    def _():
        for z in range(half):
            f_copy(z).wait_send()


def local(c_states, velocity):
    intervals = lax.axis_size("tm")
    slabs = lax.axis_size("gz")
    zs, rows, y_all = velocity.shape[1:]
    core = y_all // slabs
    depth = zs * slabs
    half = depth // 2
    halo = 2 * STEPS + 2 * (intervals - 1)
    lanes = min(y_all, -(-(core + 2 * halo) // LANES) * LANES)
    offset = (lanes - core) // 4 * 2
    f32 = jnp.float32
    windows = pltpu.VMEM((slabs, 3, zs, rows, lanes), f32)
    field = pltpu.VMEM((3, depth + 2, rows, lanes), f32)
    coarse = pltpu.VMEM((3, half + 2, rows // 2, lanes), f32)
    flat = pltpu.VMEM((half, 3, rows // 2, lanes), f32)
    layered = pltpu.SemaphoreType.DMA((half,))
    several = pltpu.SemaphoreType.DMA((slabs,))
    return pl.pallas_call(
        functools.partial(kernel, intervals, slabs, offset),
        out_shape=jax.ShapeDtypeStruct(c_states.shape, f32),
        in_specs=[pl.BlockSpec(memory_space=pl.ANY)] * 2,
        out_specs=pl.BlockSpec(memory_space=pltpu.VMEM),
        scratch_shapes=[
            pltpu.VMEM(c_states.shape, f32),
            pltpu.VMEM(velocity.shape, f32),
            windows, windows, field, field, field, field,
            pltpu.VMEM((15, depth, rows, lanes), f32),
            coarse,
            pltpu.VMEM((15, half, rows // 2, lanes), f32),
            pltpu.VMEM((lanes // LANES, 3, half, rows, LANES), f32),
            coarse, coarse, coarse, flat, flat,
            windows,
            pltpu.VMEM((slabs, 3, zs // 2, rows // 2, lanes), f32),
            pltpu.VMEM((y_all // LANES, 3, zs // 2, rows, LANES), f32),
            pltpu.SemaphoreType.DMA((2,)),
            several, several, several, several, several, several, several, several,
            several, several, several, several,
            layered, layered,
        ],
        compiler_params=pltpu.CompilerParams(
            collective_id=0, has_side_effects=True, vmem_limit_bytes=56 * 2**20
        ),
    )(c_states, velocity)


def solution(mesh):
    return jax.shard_map(
        local,
        mesh=mesh,
        in_specs=(P("tm", None, "gz", None, None), P(None, "gz", None, None)),
        out_specs=P("tm", None, "gz", None, None),
        check_vma=False,
    )
```

```python
import functools

import jax
import jax.numpy as jnp
from jax import lax
from jax.experimental import pallas as pl
from jax.experimental.pallas import tpu as pltpu
from jax.sharding import PartitionSpec as P

STEPS = 4
KAPPA = 0.04
LANES = 128
MESH = pl.DeviceIdType.MESH


def loop(n, body, most):
    width = max(d for d in range(1, max(most, 1) + 1) if n % d == 0)

    def block(first):
        lax.fori_loop(0, width, lambda k, carry: (body(first + k), carry)[1], 0, unroll=True)

    if width == n:
        block(0)
    else:
        lax.fori_loop(0, n // width, lambda b, carry: (block(b * width), carry)[1], 0)


def kernel(
    intervals, slabs, offset,
    c_hbm, v_hbm, out_ref,
    c_ref, v_ref, v_win, c_win, speed, field_a, field_b, relaxed, cf, speed_c, cf_c,
    pairs, r_relaxed, r_again, delta, sent, got, rel_slab, delta_slab, fine_tmp,
    in_sem, v_send, v_recv, s_send, s_recv, c_send, c_recv, w_send, w_recv, r_send, r_recv, d_send, d_recv, f_send, f_recv,
):
    t = lax.axis_index("tm")
    me = lax.axis_index("gz")
    first_t = t == 0
    last_t = t == intervals - 1
    zs, rows, y_all = v_ref.shape[1:]
    core = y_all // slabs
    depth = zs * slabs
    half = depth // 2
    zsc = zs // 2
    lanes = v_win.shape[-1]
    wide = 16 * LANES // lanes

    v_in = pltpu.make_async_copy(v_hbm, v_ref, in_sem.at[0])
    c_in = pltpu.make_async_copy(c_hbm, c_ref, in_sem.at[1])
    v_in.start()
    c_in.start()
    core_index = t % 2
    sibling = t + 1 - 2 * core_index

    barrier = pltpu.get_barrier_semaphore()
    for g in range(slabs):
        @pl.when(me != g)
        def _():
            pl.semaphore_signal(barrier, inc=1, device_id=(t, g), device_id_type=MESH)

        @pl.when(jnp.logical_not(first_t))
        def _():
            pl.semaphore_signal(barrier, inc=1, device_id=(t - 1, g), device_id_type=MESH)

        @pl.when(jnp.logical_not(last_t))
        def _():
            pl.semaphore_signal(barrier, inc=1, device_id=(t + 1, g), device_id_type=MESH)

    def cut(read, target):
        def layer(z):
            for c in range(3):
                whole = read(c, z)
                for g in range(slabs):
                    shift = (offset - g * core) % y_all
                    turned = pltpu.roll(whole, shift, 1) if shift else whole
                    target[g, c, z] = turned[:, :lanes]

        loop(zs, layer, 16 // slabs)

    v_in.wait()
    cut(lambda c, z: v_ref[c, z], v_win)
    nothing = jnp.zeros((rows, lanes), jnp.float32)
    nothing_c = jnp.zeros((rows // 2, lanes), jnp.float32)
    for c in range(3):
        for ref in (speed, field_a, field_b, relaxed):
            ref[c, 0] = nothing
            ref[c, depth + 1] = nothing
        for ref in (speed_c, delta):
            ref[c, 0] = nothing_c
            ref[c, half + 1] = nothing_c

    sides = 2 - first_t.astype(jnp.int32) - last_t.astype(jnp.int32)
    pl.semaphore_wait(barrier, slabs - 1 + slabs * sides)

    def slab_of(ref, g, width):
        return ref.at[:, pl.ds(1 + g * width, width)]

    def v_copy(g, slot):
        return pltpu.make_async_remote_copy(
            v_win.at[g, :, pl.ds(core_index * zsc, zsc)],
            speed.at[:, pl.ds(1 + slot * zs + core_index * zsc, zsc)],
            v_send.at[g], v_recv.at[slot],
            device_id=(t, g), device_id_type=MESH)

    def s_copy(slot, which):
        layers = speed.at[:, pl.ds(1 + slot * zs + which * zsc, zsc)]
        return pltpu.make_async_remote_copy(
            layers, layers, s_send.at[slot], s_recv.at[slot],
            device_id=(sibling, me), device_id_type=MESH)

    def c_copy(g, slot):
        return pltpu.make_async_remote_copy(
            c_win.at[g], slab_of(field_a, slot, zs), c_send.at[g], c_recv.at[slot],
            device_id=(t + 1, g), device_id_type=MESH)

    def w_copy(slot):
        return pltpu.make_async_remote_copy(
            slab_of(field_a, slot, zs), slab_of(relaxed, slot, zs), w_send.at[slot], w_recv.at[slot],
            device_id=(sibling, me), device_id_type=MESH)

    def r_copy(g, slot):
        return pltpu.make_async_remote_copy(
            slab_of(relaxed, g, zs), rel_slab.at[slot], r_send.at[g], r_recv.at[slot],
            device_id=(t, g), device_id_type=MESH)

    def d_copy(g, slot):
        return pltpu.make_async_remote_copy(
            slab_of(delta, g, zsc), delta_slab.at[slot], d_send.at[g], d_recv.at[slot],
            device_id=(t, g), device_id_type=MESH)

    def f_copy(z):
        return pltpu.make_async_remote_copy(
            sent.at[z], got.at[z], f_send.at[z], f_recv.at[z],
            device_id=(t + 1, me), device_id_type=MESH)

    def ahead(d):
        return lax.rem(me + d, slabs)

    for d in range(1, slabs):
        v_copy(ahead(d), me).start()

    c_in.wait()
    cut(lambda c, z: c_ref[0, c, z], c_win)
    @pl.when(jnp.logical_not(last_t))
    def _():
        for d in range(1, slabs + 1):
            c_copy(ahead(d), me).start()

    for g in range(slabs):
        @pl.when(me == g)
        def _():
            speed[:, 1 + g * zs : 1 + (g + 1) * zs] = v_win[g]

    lane = lax.broadcasted_iota(jnp.int32, (rows, lanes), 1)
    even = lane % 2 == 0
    cell = lax.rem(lane + me * core - offset + y_all, y_all)

    def coefficients(vel, cf, n, ys):
        height = vel.shape[-2]
        row = lax.broadcasted_iota(jnp.int32, (height, lanes), 0)
        y = cell[:height]
        x_low = (row > 0).astype(jnp.float32)
        x_high = (row < height - 1).astype(jnp.float32)
        y_low = (y >= ys).astype(jnp.float32)
        y_high = (y < y_all - ys).astype(jnp.float32)

        def layer(z):
            u = [vel[d, z + 1] for d in range(3)]
            low = [jnp.maximum(a, 0.0) + KAPPA for a in u]
            high = [KAPPA - jnp.minimum(a, 0.0) for a in u]
            cf[0, z] = low[0]
            cf[1, z] = high[0]
            cf[2, z] = low[1] * x_low
            cf[3, z] = high[1] * x_high
            cf[4, z] = low[2] * y_low
            cf[5, z] = high[2] * y_high
            centre = (1.0 - 6.0 * KAPPA) - (jnp.abs(u[0]) + jnp.abs(u[1]) + jnp.abs(u[2]))
            for c in range(3):
                grad = [
                    (vel[c, z + 2] - vel[c, z]) * 0.5,
                    (pltpu.roll(u[c], height - 1, 0) * x_high - pltpu.roll(u[c], 1, 0) * x_low) * 0.5,
                    (pltpu.roll(u[c], lanes - ys, 1) * y_high - pltpu.roll(u[c], ys, 1) * y_low) * 0.5,
                ]
                for d in range(3):
                    cf[6 + 3 * c + d, z] = grad[d] + centre if d == c else grad[d]

        loop(n, layer, wide)

    def march_layer(src, put, cf, z, ys, extra=None):
        height = src.shape[-2]
        w = [src[c, z + 1] for c in range(3)]
        a = [cf[i, z] for i in range(6)]
        for c in range(3):
            new = cf[6 + 3 * c, z] * w[0] + cf[7 + 3 * c, z] * w[1] + cf[8 + 3 * c, z] * w[2]
            new = new + (a[0] * src[c, z] + a[1] * src[c, z + 2])
            new = new + (a[2] * pltpu.roll(w[c], 1, 0) + a[3] * pltpu.roll(w[c], height - 1, 0))
            new = new + (a[4] * pltpu.roll(w[c], ys, 1) + a[5] * pltpu.roll(w[c], lanes - ys, 1))
            put(c, new)

    def march(src, dst, n, unroll):
        def layer(z):
            def put(c, new):
                dst[c, z + 1] = new

            march_layer(src, put, cf, z, 1)

        loop(n, layer, unroll)

    def restrict(src, dst, scale):
        def layer(z):
            for c in range(3):
                both = src[c, 2 * z + 1] + src[c, 2 * z + 2]
                both = both + jnp.where(even, pltpu.roll(both, lanes - 1, 1), pltpu.roll(both, 1, 1))
                for part in range(lanes // LANES):
                    at = slice(part * LANES, (part + 1) * LANES)
                    pairs[part, c, z] = both[:, at]
            for c in range(3):
                for part in range(lanes // LANES):
                    at = slice(part * LANES, (part + 1) * LANES)
                    dst[c, z + 1, :, at] = scale * (
                        pairs[part, c, z, pl.ds(0, rows // 2, stride=2), :]
                        + pairs[part, c, z, pl.ds(1, rows // 2, stride=2), :])

        loop(half, layer, wide)

    for d in range(1, slabs):
        g = ahead(slabs - d)
        v_copy(g, g).wait_recv()
        s_copy(g, core_index).start()

    for d in range(1, slabs):
        s_copy(ahead(slabs - d), 1 - core_index).wait_recv()

    coefficients(speed, cf, depth, 1)
    restrict(speed, speed_c, 0.25)
    coefficients(speed_c, cf_c, half, 2)

    @pl.when(first_t)
    def _():
        for g in range(slabs):
            w_copy(g).wait_recv()

    @pl.when(jnp.logical_not(first_t))
    def _():
        for d in range(1, slabs + 1):
            g = ahead(slabs - d)
            c_copy(g, g).wait_recv()

            @pl.when(t == 1)
            def _():
                w_copy(g).start()

        march(field_a, field_b, depth, wide)

        @pl.when(t == 1)
        def _():
            for g in range(slabs):
                w_copy(g).wait_send()

        march(field_b, field_a, depth, wide)
        march(field_a, field_b, depth, wide)
        march(field_b, relaxed, depth, wide)

    for d in range(1, slabs):
        r_copy(ahead(d), me).start()

    for g in range(slabs):
        @pl.when(me == g)
        def _():
            rel_slab[g] = relaxed[:, 1 + g * zs : 1 + (g + 1) * zs]

    march(relaxed, field_b, depth, wide)
    march(field_b, field_a, depth, wide)
    march(field_a, field_b, depth, wide)
    march(field_b, field_a, depth, wide)
    restrict(field_a, r_again, 0.125)
    restrict(relaxed, r_relaxed, 0.125)

    @pl.when(first_t)
    def _():
        delta[:, 1 : half + 1] = jnp.zeros((3, half, rows // 2, lanes), jnp.float32)

    def send_on(z):
        @pl.when(jnp.logical_not(last_t))
        def _():
            def put(c, new):
                sent[z, c] = new + r_again[c, z + 1]

            march_layer(delta, put, cf_c, z, 2)
            f_copy(z).start()

    for z in range(half):
        @pl.when(jnp.logical_not(first_t))
        def _():
            f_copy(z).wait_recv()
            delta[:, z + 1] = got[z] - r_relaxed[:, z + 1]

        if z > 0:
            send_on(z - 1)
        if z % zsc == zsc - 1:
            g = z // zsc

            @pl.when(me != g)
            def _():
                d_copy(g, me).start()

            @pl.when(me == g)
            def _():
                delta_slab[g] = delta[:, 1 + g * zsc : 1 + (g + 1) * zsc]
    send_on(half - 1)

    tile_lane = lax.broadcasted_iota(jnp.int32, (rows, LANES), 1)

    def joined(read, tile):
        total = None
        for g in range(slabs):
            start = g * core - tile * LANES
            if start < 0 or start >= LANES:
                continue
            shift = (start - offset) % lanes
            piece = read(g)
            piece = pltpu.roll(piece, shift, 1) if shift else piece
            piece = piece[:, :LANES]
            total = piece if total is None else jnp.where(tile_lane[: piece.shape[0]] >= start, piece, total)
        return total

    for g in range(slabs):
        @pl.when(me != g)
        def _():
            r_copy(g, g).wait_recv()

    def rel_layer(z):
        for c in range(3):
            for tile in range(y_all // LANES):
                out_ref[0, c, z, :, tile * LANES : (tile + 1) * LANES] = joined(lambda g: rel_slab[g, c, z], tile)

    loop(zs, rel_layer, zs)

    for g in range(slabs):
        @pl.when(me != g)
        def _():
            d_copy(g, g).wait_recv()

    def out_layer(z):
        for c in range(3):
            for tile in range(y_all // LANES):
                at = slice(tile * LANES, (tile + 1) * LANES)
                coarse = joined(lambda g: delta_slab[g, c, z], tile)
                fine_tmp[tile, c, z, pl.ds(0, rows // 2, stride=2), :] = coarse
                fine_tmp[tile, c, z, pl.ds(1, rows // 2, stride=2), :] = coarse
            for tile in range(y_all // LANES):
                at = slice(tile * LANES, (tile + 1) * LANES)
                fine = fine_tmp[tile, c, z]
                for k in range(2):
                    out_ref[0, c, 2 * z + k, :, at] = out_ref[0, c, 2 * z + k, :, at] + fine

    loop(zsc, out_layer, zsc)

    for g in range(slabs):
        @pl.when(me != g)
        def _():
            v_copy(g, me).wait_send()
            s_copy(g, core_index).wait_send()
            r_copy(g, me).wait_send()
            d_copy(g, me).wait_send()

        @pl.when(jnp.logical_not(last_t))
        def _():
            c_copy(g, me).wait_send()

    @pl.when(jnp.logical_not(last_t))
    def _():
        for z in range(half):
            f_copy(z).wait_send()


def local(c_states, velocity):
    intervals = lax.axis_size("tm")
    slabs = lax.axis_size("gz")
    zs, rows, y_all = velocity.shape[1:]
    core = y_all // slabs
    depth = zs * slabs
    half = depth // 2
    halo = 2 * STEPS + 2 * (intervals - 1)
    lanes = min(y_all, -(-(core + 2 * halo) // LANES) * LANES)
    offset = (lanes - core) // 4 * 2
    f32 = jnp.float32
    windows = pltpu.VMEM((slabs, 3, zs, rows, lanes), f32)
    field = pltpu.VMEM((3, depth + 2, rows, lanes), f32)
    coarse = pltpu.VMEM((3, half + 2, rows // 2, lanes), f32)
    flat = pltpu.VMEM((half, 3, rows // 2, lanes), f32)
    layered = pltpu.SemaphoreType.DMA((half,))
    several = pltpu.SemaphoreType.DMA((slabs,))
    return pl.pallas_call(
        functools.partial(kernel, intervals, slabs, offset),
        out_shape=jax.ShapeDtypeStruct(c_states.shape, f32),
        in_specs=[pl.BlockSpec(memory_space=pl.ANY)] * 2,
        out_specs=pl.BlockSpec(memory_space=pltpu.VMEM),
        scratch_shapes=[
            pltpu.VMEM(c_states.shape, f32),
            pltpu.VMEM(velocity.shape, f32),
            windows, windows, field, field, field, field,
            pltpu.VMEM((15, depth, rows, lanes), f32),
            coarse,
            pltpu.VMEM((15, half, rows // 2, lanes), f32),
            pltpu.VMEM((lanes // LANES, 3, half, rows, LANES), f32),
            coarse, coarse, coarse, flat, flat,
            windows,
            pltpu.VMEM((slabs, 3, zs // 2, rows // 2, lanes), f32),
            pltpu.VMEM((y_all // LANES, 3, zs // 2, rows, LANES), f32),
            pltpu.SemaphoreType.DMA((2,)),
            several, several, several, several, several, several, several, several,
            several, several, several, several,
            layered, layered,
        ],
        compiler_params=pltpu.CompilerParams(
            collective_id=0, has_side_effects=True, vmem_limit_bytes=56 * 2**20
        ),
    )(c_states, velocity)


def solution(mesh):
    return jax.shard_map(
        local,
        mesh=mesh,
        in_specs=(P("tm", None, "gz", None, None), P(None, "gz", None, None)),
        out_specs=P("tm", None, "gz", None, None),
        check_vma=False,
    )
```
